512 devices in a mesh: gx: 4 (over y_hi), ea: 128 (over y_lo, z, x, core).
Axes of the slice: x: 4, y: 8 (y_hi: 4, y_lo: 2; y = y_hi * 2 + y_lo), z: 8, core: 2. Of those that a mesh axis runs over, the one named last changes fastest.
Arguments:
- ham_diag: float32 [2, 4, 128, 128], P(None, 'gx'), may hold values from -2 to 2, as said below
- ham_coupling: float32 [2, 4, 128, 128], P(None, 'gx'), may hold values from -0.25 to 0.25
- sigma_prev: float32 [2, 4, 128, 128, 128], P(None, 'gx', 'ea'), may hold values from -0.5 to 0.5, as said below
- phonon_form: float32 [128, 128], replicated, may hold values from 0.05 to 0.5
- contact_rate: float32 [2, 128, 128], P(None, 'ea'), may hold values from 0.2 to 2
Outputs:
- sigma_next: float32 [2, 4, 128, 128, 128], P(None, 'gx', 'ea')
The draws below stay inside these ranges and needn't reach their ends.
Inputs may be any that keep to these rules, and one draw needn't show every extreme that they name: `ham_diag`: each block is Hermitian: real part symmetric, imaginary part antisymmetric. `sigma_prev`: for every block, (S - S^H) / (2 j) is negative definite.
All inputs are finite; a program needn't handle non-finite values.
Results may differ from the reference program's by a relative error of at most 0.0003.
Values sent between devices are 32-bit elements; how exact they have to be, the bound alone decides.
A program may use at most 64 MiB of HBM per device.

```python
import math
import jax
import jax.numpy as jnp
from jax import lax

ORB = 128
E_DEV = 1
SLICES = 4
ENERGIES = 128


def symmetric_part(values):
    return 0.5 * (values + jnp.swapaxes(values, -1, -2))


def antisymmetric_part(values):
    return 0.5 * (values - jnp.swapaxes(values, -1, -2))


def draw_ham_diag(key, part):
    key = jax.random.fold_in(key, 11)
    keys = jax.random.split(key, 3)
    shape = (SLICES, ORB, ORB)
    first = jax.random.truncated_normal(keys[0], -4.0, 4.0, shape, jnp.float32)
    second = jax.random.truncated_normal(keys[1], -4.0, 4.0, shape, jnp.float32)
    onsite = jax.random.uniform(keys[2], (SLICES, ORB), jnp.float32, -1.0, 1.0)
    scale = 0.6 * (2.0 / ORB) ** 0.5
    identity = jnp.eye(ORB, dtype=jnp.float32)
    real_part = symmetric_part(first) * scale + onsite[:, :, None] * identity
    imaginary = antisymmetric_part(second) * scale
    return jnp.stack([real_part, imaginary])


def draw_sigma_prev(key, part):
    key = jax.random.fold_in(key, 23)
    keys = jax.random.split(key, 4)
    shape = (SLICES, ENERGIES, ORB, ORB)
    first = jax.random.truncated_normal(keys[0], -4.0, 4.0, shape, jnp.float32)
    second = jax.random.truncated_normal(keys[1], -4.0, 4.0, shape, jnp.float32)
    rate = jnp.exp(jax.random.uniform(keys[2], (SLICES, ENERGIES, ORB), jnp.float32, jnp.log(0.03), jnp.log(0.15)))
    spread = jax.random.uniform(keys[3], shape, jnp.float32, -1.0, 1.0) * (0.02 / ORB)
    scale = 0.25 * (2.0 / ORB) ** 0.5
    identity = jnp.eye(ORB, dtype=jnp.float32)
    damping = rate[..., None] * identity + symmetric_part(spread)
    real_part = symmetric_part(first) * scale
    imaginary = antisymmetric_part(second) * scale - damping
    return jnp.stack([real_part, imaginary])


def levels(stream_key, extent, cuts, least, high):
    def one(axis_at, blocks):
        steps = jax.random.uniform(jax.random.fold_in(jax.random.fold_in(stream_key, 6), axis_at), (blocks,), jnp.float32, least / len(cuts), high / len(cuts))
        return jnp.repeat(jnp.exp(steps), extent[axis_at] // blocks).reshape((-1,) + (1,) * (len(extent) - axis_at - 1))

    level = one(*cuts[0])
    for cut in cuts[1:]:
        level = level * one(*cut)
    return level


def scatter_about(own_key, shape, scale, reach, shards=(), held_as=jnp.bfloat16):
    values = scale * jax.random.normal(own_key, shape, jnp.float32)
    if shards:
        values = values * levels(own_key, shape, shards, -0.22, 0.18)
    return jnp.clip(values, -reach, reach).astype(held_as)


def setup_inputs(seed: int = 0) -> dict:
    splits = jax.random.split(jax.random.key(seed), 6)
    return {
        "ham_diag": draw_ham_diag(jax.random.fold_in(splits[5], 71), 0),
        "ham_coupling": scatter_about(splits[1], (2, SLICES, ORB, ORB), (4 * ORB) ** -0.5, 0.25, ((1, 4),), jnp.float32),
        "sigma_prev": draw_sigma_prev(jax.random.fold_in(splits[5], 71), 0),
        "phonon_form": jnp.clip(jnp.exp(jax.random.uniform(splits[3], (ORB, ORB), jnp.float32, math.log(0.05), math.log(0.5))), 0.05, 0.5),
        "contact_rate": jnp.clip(jnp.exp(math.log(2.0) - 2.3025851 * jax.random.uniform(splits[4], (2, ENERGIES, ORB), jnp.float32) ** levels(splits[4], (2, ENERGIES, ORB), ((1, 128),), -0.2, 0.2)), 0.2, 2.0),
    }


BROADENING = 0.05
ENERGY_LOW = -2.0
ENERGY_SPAN = 4.0

def product_real(left, right):
    return jnp.matmul(left, right, precision=lax.Precision.HIGHEST)

def multiply(left, right):
    return (product_real(left[0], right[0]) - product_real(left[1], right[1]), product_real(left[0], right[1]) + product_real(left[1], right[0]))

def addition(left, right):
    return (left[0] + right[0], left[1] + right[1])

def subtract(left, right):
    return (left[0] - right[0], left[1] - right[1])

def adjoint(pair):
    return (jnp.swapaxes(pair[0], -1, -2), -jnp.swapaxes(pair[1], -1, -2))

def sandwich(left, middle, right):
    return multiply(multiply(left, middle), right)

def invert(matrix):
    dimension = matrix[0].shape[-1]
    upper_rows = jnp.concatenate([matrix[0], -matrix[1]], axis=1)
    lower_rows = jnp.concatenate([matrix[1], matrix[0]], axis=1)
    embedded = jnp.concatenate([upper_rows, lower_rows], axis=0)
    right_side = jnp.concatenate([jnp.eye(dimension, dtype=matrix[0].dtype), jnp.zeros((dimension, dimension), matrix[0].dtype)], axis=0)
    solution = jnp.linalg.solve(embedded, right_side)
    return (solution[:dimension], solution[dimension:])

def green_diagonal(ham_diag, ham_coupling, sigma_energy, rate_energy, energy):
    identity = jnp.eye(ORB, dtype=jnp.float32)
    real_part = energy * identity - ham_diag[0] - sigma_energy[0]
    imaginary = BROADENING * identity - ham_diag[1] - sigma_energy[1]
    imaginary = imaginary.at[0].add(rate_energy[0][:, None] * identity)
    imaginary = imaginary.at[SLICES - 1].add(rate_energy[1][:, None] * identity)
    links_real = ham_coupling[0][:SLICES - 1]
    links_imag = ham_coupling[1][:SLICES - 1]
    first_green = invert((real_part[0], imaginary[0]))

    def forward(carry, item):
        link = (item[2], item[3])
        pivot_block = subtract((item[0], item[1]), sandwich(adjoint(link), carry, link))
        green = invert(pivot_block)
        return (green, green)
    last_green, later = lax.scan(forward, first_green, (real_part[1:], imaginary[1:], links_real, links_imag))
    left_real = jnp.concatenate([first_green[0][None], later[0]], axis=0)
    left_imag = jnp.concatenate([first_green[1][None], later[1]], axis=0)

    def backward(carry, item):
        green = (item[0], item[1])
        link = (item[2], item[3])
        partial_row = multiply(multiply(green, link), carry)
        value = addition(green, multiply(multiply(partial_row, adjoint(link)), green))
        return (value, value)
    final_carry, earlier = lax.scan(backward, last_green, (left_real[:-1], left_imag[:-1], links_real, links_imag), reverse=True)
    diag_real = jnp.concatenate([earlier[0], last_green[0][None]], axis=0)
    diag_imag = jnp.concatenate([earlier[1], last_green[1][None]], axis=0)
    return jnp.stack([diag_real, diag_imag])

def reference(ham_diag, ham_coupling, sigma_prev, phonon_form, contact_rate):
    energies = ENERGY_LOW + ENERGY_SPAN * (jnp.arange(ENERGIES, dtype=jnp.float32) + 0.5) / ENERGIES

    def one_energy(item):
        return green_diagonal(ham_diag, ham_coupling, item[0], item[1], item[2])
    greens = lax.map(one_energy, (jnp.moveaxis(sigma_prev, 2, 0), jnp.moveaxis(contact_rate, 1, 0), energies))
    greens = jnp.moveaxis(greens, 0, 2)
    padding = jnp.zeros(greens.shape[:2] + (E_DEV,) + greens.shape[3:], greens.dtype)
    padded = jnp.concatenate([padding, greens, padding], axis=2)
    return phonon_form * (padded[:, :, :ENERGIES] + padded[:, :, 2 * E_DEV:])
```

```python
import jax
import jax.numpy as jnp
from jax import lax
from jax.experimental import pallas as pl
from jax.experimental.pallas import tpu as pltpu
from jax.sharding import PartitionSpec as P

BROADENING = 0.05
ENERGY_LOW = -2.0
ENERGY_SPAN = 4.0
N = 128
TILE = (8, 128)
MESH = pl.DeviceIdType.MESH


def spread(x):
    return jnp.broadcast_to(x, TILE)


def split3(x):
    high = x.astype(jnp.bfloat16)
    rest = x - high.astype(jnp.float32)
    middle = rest.astype(jnp.bfloat16)
    low = (rest - middle.astype(jnp.float32)).astype(jnp.bfloat16)
    return high, middle, low


def dot16(a, b):
    return jnp.dot(a, b, preferred_element_type=jnp.float32)


def product6(left, right):
    lh, lm, ll = left
    rh, rm, rl = right
    small = (dot16(lm, rm) + dot16(lh, rl)) + dot16(ll, rh)
    return dot16(lh, rh) + ((dot16(lh, rm) + dot16(lm, rh)) + small)


def multiply(left, right):
    x = jnp.concatenate(left, axis=1)
    top = jnp.concatenate(right, axis=1)
    bottom = jnp.concatenate([-right[1], right[0]], axis=1)
    y = product6(split3(x), split3(jnp.concatenate([top, bottom], axis=0)))
    return y[:, :N], y[:, N:]


def adjoint(pair):
    return pair[0].T, -pair[1].T


def addition(left, right):
    return left[0] + right[0], left[1] + right[1]


def subtract(left, right):
    return left[0] - right[0], left[1] - right[1]


def pair_of(ref):
    return ref[0], ref[1]


def store(ref, pair):
    ref[0] = pair[0]
    ref[1] = pair[1]


def pivot_rows(t, rows):
    sub = lax.broadcasted_iota(jnp.int32, TILE, 0)
    lane = lax.broadcasted_iota(jnp.int32, TILE, 1)
    o = 8 * t
    cols = [(spread(rows[0][:, o + m : o + m + 1]), spread(rows[1][:, o + m : o + m + 1])) for m in range(8)]
    inside = (lane >= o) & (lane < o + 8)
    x = (
        jnp.where(inside, jnp.where(lane - o == sub, 1.0, 0.0), rows[0]),
        jnp.where(inside, 0.0, rows[1]),
    )
    for k in range(8):
        at = sub == k
        mr, mi = cols[k]
        pr, pi = spread(mr[k : k + 1]), spread(mi[k : k + 1])
        recip = 1.0 / (pr * pr + pi * pi)
        mr, mi = jnp.where(at, -1.0, mr), jnp.where(at, 0.0, mi)
        ur, ui = mr * pr + mi * pi, mi * pr - mr * pi
        wr, wi = ur * recip, ui * recip

        def step(v, next_pivot):
            rr, ri = spread(v[0][k : k + 1]), spread(v[1][k : k + 1])
            vr, vi = jnp.where(at, 0.0, v[0]), jnp.where(at, 0.0, v[1])
            if next_pivot:
                return vr - (ur * rr - ui * ri) * recip, vi - (ur * ri + ui * rr) * recip
            return vr - (wr * rr - wi * ri), vi - (wr * ri + wi * rr)

        for m in range(k + 1, 8):
            cols[m] = step(cols[m], m == k + 1)
        x = step(x, False)
    return x


def eliminate(rows, t, x):
    lane = lax.broadcasted_iota(jnp.int32, TILE, 1)
    o = 8 * t
    inside = (lane >= o) & (lane < o + 8)
    real, imag = [], []
    for k in range(8):
        cr, ci = spread(rows[0][:, o + k : o + k + 1]), spread(rows[1][:, o + k : o + k + 1])
        rr, ri = spread(x[0][k : k + 1]), spread(x[1][k : k + 1])
        real.append(cr * rr - ci * ri)
        imag.append(cr * ri + ci * rr)
    while len(real) > 1:
        real = [a + b for a, b in zip(real[::2], real[1::2])]
        imag = [a + b for a, b in zip(imag[::2], imag[1::2])]
    return jnp.where(inside, 0.0, rows[0]) - real[0], jnp.where(inside, 0.0, rows[1]) - imag[0]


def invert(ref):
    groups = N // 8
    a = [(ref[0, 8 * g : 8 * g + 8, :], ref[1, 8 * g : 8 * g + 8, :]) for g in range(groups)]
    lane = lax.broadcasted_iota(jnp.int32, TILE, 1)
    for s in range(groups // 2):
        g0, g1 = 2 * s, 2 * s + 1
        ahead = [] if s == groups // 2 - 1 else [g1 + 1, g1 + 2]
        old = list(a)
        x0 = pivot_rows(g0, a[g0])
        second = eliminate(a[g1], g0, x0)
        early = [eliminate(a[h], g0, x0) for h in ahead]
        x1 = pivot_rows(g1, second)
        early = [eliminate(h, g1, x1) for h in early]
        x0 = eliminate(x0, g1, x1)
        a[g0], a[g1] = x0, x1
        for h, v in zip(ahead, early):
            a[h] = v
        done = [g0, g1] + ahead
        real = jnp.concatenate([x0[0], x1[0]], axis=0)
        imag = jnp.concatenate([x0[1], x1[1]], axis=0)
        top = split3(jnp.concatenate([real, imag], axis=1))
        bottom = split3(jnp.concatenate([-imag, real], axis=1))

        def placed(x):
            above = [jnp.zeros((16 * s, 2 * N), jnp.bfloat16)] if s else []
            below = [jnp.zeros((N - 16 * s - 16, 2 * N), jnp.bfloat16)] if ahead else []
            return above + [x] + below

        right = [jnp.concatenate(placed(u) + placed(v), axis=0) for u, v in zip(top, bottom)]
        left = jnp.concatenate(
            [jnp.concatenate([v[0] for v in old], axis=0), jnp.concatenate([v[1] for v in old], axis=0)], axis=1
        )
        change = product6(split3(left), right)
        inside = (lane >= 16 * s) & (lane < 16 * s + 16)
        for g in range(groups):
            if g not in done:
                rows = slice(8 * g, 8 * g + 8)
                a[g] = (
                    jnp.where(inside, 0.0, old[g][0]) - change[rows, :N],
                    jnp.where(inside, 0.0, old[g][1]) - change[rows, N:],
                )
    for g in range(groups):
        ref[0, 8 * g : 8 * g + 8, :] = a[g][0]
        ref[1, 8 * g : 8 * g + 8, :] = a[g][1]


def kernel(
    diag_ref, coupling_ref, sigma_ref, form_ref, rate_ref, out_ref,
    own, work, near, link, mid, link_h, one, gv, vg, sent, far, last, before, after,
    send_sem, recv_sem,
):
    gx = lax.axis_index("gx")
    ea = lax.axis_index("ea")
    count = lax.axis_size("ea")
    left = gx < 2
    outer = (gx == 0) | (gx == 3)
    inner = jnp.logical_not(outer)
    partner = gx + 1 - 2 * lax.rem(gx, 2)
    across = 3 - gx
    beyond = lax.rem(gx + 2, 4)

    def copy(src, dst, at, to_gx, to_ea, landed=None):
        return pltpu.make_async_remote_copy(
            src_ref=src,
            dst_ref=dst,
            send_sem=send_sem.at[at],
            recv_sem=recv_sem.at[at if landed is None else landed],
            device_id=(to_gx, to_ea),
            device_id_type=MESH,
        )

    send_near = copy(own, near, 0, partner, ea)
    send_link = copy(coupling_ref.at[:, 0], link, 1, partner, ea)
    send_mid = copy(sent, mid, 2, partner, ea)
    send_across = copy(sent, far, 3, across, ea)
    send_beyond = copy(sent, far, 4, beyond, ea, 3)
    send_up = copy(last, before, 5, gx, lax.rem(ea + 1, count))
    send_down = copy(last, after, 6, gx, lax.rem(ea + count - 1, count))

    barrier = pltpu.get_barrier_semaphore()

    def greet(to_gx, to_ea):
        pl.semaphore_signal(barrier, inc=1, device_id=(to_gx, to_ea), device_id_type=MESH)

    greet(partner, ea)
    greet(beyond, ea)

    @pl.when(outer)
    def _():
        greet(across, ea)

    @pl.when(ea > 0)
    def _():
        greet(gx, ea - 1)

    @pl.when(ea < count - 1)
    def _():
        greet(gx, ea + 1)

    row = lax.broadcasted_iota(jnp.int32, (N, N), 0)
    column = lax.broadcasted_iota(jnp.int32, (N, N), 1)
    energy = ENERGY_LOW + ENERGY_SPAN * (ea.astype(jnp.float32) + 0.5) / count
    first = jnp.where(gx == 0, 1.0, 0.0)
    final = jnp.where(gx == 3, 1.0, 0.0)
    rate = BROADENING + (first * rate_ref[0] + final * rate_ref[1])
    on_diagonal = row == column
    own[0] = jnp.where(on_diagonal, energy, 0.0) - diag_ref[0, 0] - sigma_ref[0, 0, 0]
    own[1] = jnp.where(on_diagonal, rate, 0.0) - diag_ref[1, 0] - sigma_ref[1, 0, 0]

    waits = jnp.where(outer, 3, 2) + jnp.where(ea > 0, 1, 0) + jnp.where(ea < count - 1, 1, 0)

    @pl.when(inner)
    def _():
        pl.semaphore_wait(barrier, waits)
        send_near.start()
        send_link.start()

    @pl.when(outer)
    def _():
        work[...] = own[...]

    def level(number, carry):
        @pl.when(outer | (number == 2))
        def _():
            invert(work)

        @pl.when(outer & (number == 0))
        def _():
            pl.semaphore_wait(barrier, waits)
            send_near.wait_recv()
            send_link.wait_recv()

            @pl.when(left)
            def _():
                store(link_h, (coupling_ref[0, 0], coupling_ref[1, 0]))
                store(one, adjoint(pair_of(link_h)))

            @pl.when(jnp.logical_not(left))
            def _():
                store(one, pair_of(link))
                store(link_h, adjoint(pair_of(link)))

            g = pair_of(work)
            store(own, g)
            reached = multiply(pair_of(one), g)
            store(vg, reached)
            pivot = subtract(pair_of(near), multiply(reached, pair_of(link_h)))
            store(work, pivot)
            store(sent, pivot)
            send_mid.start()
            store(mid, pivot)
            store(gv, multiply(g, pair_of(link_h)))

        @pl.when(outer & (number == 1))
        def _():
            send_mid.wait_send()

            @pl.when(left)
            def _():
                u = pair_of(link)
                store(sent, multiply(adjoint(u), multiply(pair_of(work), u)))

            @pl.when(jnp.logical_not(left))
            def _():
                store(sent, pair_of(work))

            send_across.start()
            send_beyond.start()
            send_across.wait_recv()

        @pl.when(inner & (number == 1))
        def _():
            send_mid.wait_recv()
            send_beyond.wait_recv()
            store(link, (coupling_ref[0, 0], coupling_ref[1, 0]))

        @pl.when(number == 1)
        def _():
            @pl.when(left)
            def _():
                u = pair_of(link)
                store(far, multiply(multiply(u, pair_of(far)), adjoint(u)))

            store(work, subtract(pair_of(mid), pair_of(far)))

        return carry

    lax.fori_loop(0, 3, level, 0)

    @pl.when(outer)
    def _():
        store(last, addition(pair_of(own), multiply(multiply(pair_of(gv), pair_of(work)), pair_of(vg))))

    @pl.when(inner)
    def _():
        store(last, pair_of(work))

    @pl.when(ea < count - 1)
    def _():
        send_up.start()

    @pl.when(ea > 0)
    def _():
        send_down.start()

    @pl.when(ea == 0)
    def _():
        before[...] = jnp.zeros_like(before)

    @pl.when(ea == count - 1)
    def _():
        after[...] = jnp.zeros_like(after)

    @pl.when(inner)
    def _():
        send_near.wait_send()
        send_link.wait_send()

    @pl.when(outer)
    def _():
        send_across.wait_send()
        send_beyond.wait_send()

    @pl.when(ea > 0)
    def _():
        send_up.wait_recv()

    @pl.when(ea < count - 1)
    def _():
        send_down.wait_recv()

    for c in range(2):
        out_ref[c, 0, 0] = form_ref[...] * (before[c] + after[c])

    @pl.when(ea < count - 1)
    def _():
        send_up.wait_send()

    @pl.when(ea > 0)
    def _():
        send_down.wait_send()


def per_device(ham_diag, ham_coupling, sigma_prev, phonon_form, contact_rate):
    block = pltpu.VMEM((2, N, N), jnp.float32)
    return pl.pallas_call(
        kernel,
        out_shape=jax.ShapeDtypeStruct(sigma_prev.shape, jnp.float32),
        in_specs=[pl.BlockSpec(memory_space=pltpu.VMEM)] * 5,
        out_specs=pl.BlockSpec(memory_space=pltpu.VMEM),
        scratch_shapes=[block] * 14
        + [pltpu.SemaphoreType.DMA((7,)), pltpu.SemaphoreType.DMA((7,))],
        compiler_params=pltpu.CompilerParams(
            collective_id=0, has_side_effects=True, vmem_limit_bytes=48 << 20
        ),
        name="born_update",
    )(ham_diag, ham_coupling, sigma_prev, phonon_form, contact_rate)


def solution(mesh):
    placed = (
        P(None, "gx", None, None),
        P(None, "gx", None, None),
        P(None, "gx", "ea", None, None),
        P(),
        P(None, "ea", None),
    )
    return jax.shard_map(
        per_device,
        mesh=mesh,
        in_specs=placed,
        out_specs=P(None, "gx", "ea", None, None),
        check_vma=False,
    )
```

```python
import jax
import jax.numpy as jnp
from jax import lax
from jax.experimental import pallas as pl
from jax.experimental.pallas import tpu as pltpu
from jax.sharding import PartitionSpec as P

BROADENING = 0.05
ENERGY_LOW = -2.0
ENERGY_SPAN = 4.0
N = 128
TILE = (8, 128)
SHARE = 8
ROWS = N // SHARE
MESH = pl.DeviceIdType.MESH


def spread(x):
    return jnp.broadcast_to(x, TILE)


def split3(x):
    high = x.astype(jnp.bfloat16)
    rest = x - high.astype(jnp.float32)
    middle = rest.astype(jnp.bfloat16)
    low = (rest - middle.astype(jnp.float32)).astype(jnp.bfloat16)
    return high, middle, low


def dot16(a, b):
    return jnp.dot(a, b, preferred_element_type=jnp.float32)


def product6(left, right):
    lh, lm, ll = left
    rh, rm, rl = right
    small = (dot16(lm, rm) + dot16(lh, rl)) + dot16(ll, rh)
    return dot16(lh, rh) + ((dot16(lh, rm) + dot16(lm, rh)) + small)


def multiply(left, right):
    x = jnp.concatenate(left, axis=1)
    top = jnp.concatenate(right, axis=1)
    bottom = jnp.concatenate([-right[1], right[0]], axis=1)
    y = product6(split3(x), split3(jnp.concatenate([top, bottom], axis=0)))
    return y[:, :N], y[:, N:]


def adjoint(pair):
    return pair[0].T, -pair[1].T


def addition(left, right):
    return left[0] + right[0], left[1] + right[1]


def subtract(left, right):
    return left[0] - right[0], left[1] - right[1]


def pair_of(ref):
    return ref[0], ref[1]


def store(ref, pair):
    ref[0] = pair[0]
    ref[1] = pair[1]


def pivot_rows(t, rows):
    sub = lax.broadcasted_iota(jnp.int32, TILE, 0)
    lane = lax.broadcasted_iota(jnp.int32, TILE, 1)
    o = 8 * t
    cols = [(spread(rows[0][:, o + m : o + m + 1]), spread(rows[1][:, o + m : o + m + 1])) for m in range(8)]
    inside = (lane >= o) & (lane < o + 8)
    x = (
        jnp.where(inside, jnp.where(lane - o == sub, 1.0, 0.0), rows[0]),
        jnp.where(inside, 0.0, rows[1]),
    )
    for k in range(8):
        at = sub == k
        mr, mi = cols[k]
        pr, pi = spread(mr[k : k + 1]), spread(mi[k : k + 1])
        recip = 1.0 / (pr * pr + pi * pi)
        mr, mi = jnp.where(at, -1.0, mr), jnp.where(at, 0.0, mi)
        ur, ui = mr * pr + mi * pi, mi * pr - mr * pi
        wr, wi = ur * recip, ui * recip

        def step(v, next_pivot):
            rr, ri = spread(v[0][k : k + 1]), spread(v[1][k : k + 1])
            vr, vi = jnp.where(at, 0.0, v[0]), jnp.where(at, 0.0, v[1])
            if next_pivot:
                return vr - (ur * rr - ui * ri) * recip, vi - (ur * ri + ui * rr) * recip
            return vr - (wr * rr - wi * ri), vi - (wr * ri + wi * rr)

        for m in range(k + 1, 8):
            cols[m] = step(cols[m], m == k + 1)
        x = step(x, False)
    return x


def factors(rows, t):
    o = 8 * t
    return [(spread(rows[0][:, o + k : o + k + 1]), spread(rows[1][:, o + k : o + k + 1])) for k in range(8)]


def combine(columns, x):
    real, imag = [], []
    for k, (cr, ci) in enumerate(columns):
        rr, ri = spread(x[0][k : k + 1]), spread(x[1][k : k + 1])
        real.append(cr * rr - ci * ri)
        imag.append(cr * ri + ci * rr)
    while len(real) > 1:
        real = [a + b for a, b in zip(real[::2], real[1::2])]
        imag = [a + b for a, b in zip(imag[::2], imag[1::2])]
    return real[0], imag[0]


def cleared(rows, first, width):
    lane = lax.broadcasted_iota(jnp.int32, TILE, 1)
    inside = (lane >= first) & (lane < first + width)
    return jnp.where(inside, 0.0, rows[0]), jnp.where(inside, 0.0, rows[1])


def invert(ref, halfway):
    groups = N // 8
    a = [(ref[0, 8 * g : 8 * g + 8, :], ref[1, 8 * g : 8 * g + 8, :]) for g in range(groups)]
    for s in range(groups // 2):
        if s == 4:
            halfway()
        g0, g1 = 2 * s, 2 * s + 1
        ahead = [] if s == groups // 2 - 1 else [g1 + 1, g1 + 2]
        old = list(a)
        x0 = pivot_rows(g0, a[g0])
        x1 = pivot_rows(g1, subtract(cleared(a[g1], 8 * g0, 8), combine(factors(a[g1], g0), x0)))
        x0 = subtract(cleared(x0, 8 * g1, 8), combine(factors(x0, g1), x1))
        for h in ahead:
            part = subtract(cleared(old[h], 16 * s, 16), combine(factors(old[h], g1), x1))
            a[h] = subtract(part, combine(factors(old[h], g0), x0))
        a[g0], a[g1] = x0, x1
        done = [g0, g1] + ahead
        real = jnp.concatenate([x0[0], x1[0]], axis=0)
        imag = jnp.concatenate([x0[1], x1[1]], axis=0)
        top = split3(jnp.concatenate([real, imag], axis=1))
        bottom = split3(jnp.concatenate([-imag, real], axis=1))

        def placed(x):
            above = [jnp.zeros((16 * s, 2 * N), jnp.bfloat16)] if s else []
            below = [jnp.zeros((N - 16 * s - 16, 2 * N), jnp.bfloat16)] if ahead else []
            return above + [x] + below

        right = [jnp.concatenate(placed(u) + placed(v), axis=0) for u, v in zip(top, bottom)]
        left = jnp.concatenate(
            [jnp.concatenate([v[0] for v in old], axis=0), jnp.concatenate([v[1] for v in old], axis=0)], axis=1
        )
        change = product6(split3(left), right)
        for g in range(groups):
            if g not in done:
                rows = slice(8 * g, 8 * g + 8)
                a[g] = subtract(cleared(old[g], 16 * s, 16), (change[rows, :N], change[rows, N:]))
    for g in range(groups):
        ref[0, 8 * g : 8 * g + 8, :] = a[g][0]
        ref[1, 8 * g : 8 * g + 8, :] = a[g][1]


def kernel(
    diag_hbm, coupling_hbm, sigma_hbm, form_hbm, rate_hbm, out_ref,
    diag, coupling, sigma, form, rates,
    own, work, near, link, mid, bridge, bridge_h, step_in, step_out, reached, sent, far, last, before, after,
    load_sem, send_sem, recv_sem, pass_sem, piece_sem,
):
    gx = lax.axis_index("gx")
    ea = lax.axis_index("ea")
    count = lax.axis_size("ea")
    left = gx < 2
    right = jnp.logical_not(left)
    outer = (gx == 0) | (gx == 3)
    inner = jnp.logical_not(outer)
    even = lax.rem(gx, 2) == 0
    odd = jnp.logical_not(even)
    partner = gx + 1 - 2 * lax.rem(gx, 2)
    across = 3 - gx
    place = lax.rem(ea, SHARE)
    base = ea - place

    def load(at, src, dst):
        return pltpu.make_async_copy(src, dst, load_sem.at[at])

    load_diag = load(0, diag_hbm, diag)
    load_sigma = load(1, sigma_hbm, sigma)
    load_rates = load(2, rate_hbm, rates)
    load_coupling = load(3, coupling_hbm, coupling)
    load_form = load(4, form_hbm, form)
    for one_load in (load_diag, load_sigma, load_rates, load_coupling, load_form):
        one_load.start()

    def copy(src, dst, at, to_gx, to_ea):
        return pltpu.make_async_remote_copy(
            src_ref=src,
            dst_ref=dst,
            send_sem=send_sem.at[at],
            recv_sem=recv_sem.at[at],
            device_id=(to_gx, to_ea),
            device_id_type=MESH,
        )

    def piece(ref, index):
        return ref.at[:, pl.ds(pl.multiple_of(index * ROWS, ROWS), ROWS), :]

    send_near = copy(own, near, 0, partner, ea)
    send_piece = copy(piece(coupling.at[:, 0], place), piece(link, place), 1, partner, ea)
    send_mid = copy(sent, mid, 2, partner, ea)
    send_across = copy(sent, far, 3, across, ea)
    send_up = copy(last, before, 4, gx, lax.rem(ea + 1, count))
    send_down = copy(last, after, 5, gx, lax.rem(ea + count - 1, count))

    def hand_on(step, owner):
        return pltpu.make_async_remote_copy(
            src_ref=piece(link, owner),
            dst_ref=piece(link, owner),
            send_sem=pass_sem.at[step],
            recv_sem=piece_sem.at[step],
            device_id=(gx, base + lax.rem(place + step, SHARE)),
            device_id_type=MESH,
        )

    barrier = pltpu.get_barrier_semaphore()

    def greet(to_gx, to_ea):
        pl.semaphore_signal(barrier, inc=1, device_id=(to_gx, to_ea), device_id_type=MESH)

    greet(partner, ea)
    greet(across, ea)
    for step in range(1, SHARE):
        greet(gx, base + lax.rem(place + step, SHARE))

    @pl.when(ea > 0)
    def _():
        greet(gx, ea - 1)

    @pl.when(ea < count - 1)
    def _():
        greet(gx, ea + 1)

    waits = 1 + SHARE + jnp.where(ea > 0, 1, 0) + jnp.where(ea < count - 1, 1, 0)

    row = lax.broadcasted_iota(jnp.int32, (N, N), 0)
    column = lax.broadcasted_iota(jnp.int32, (N, N), 1)
    energy = ENERGY_LOW + ENERGY_SPAN * (ea.astype(jnp.float32) + 0.5) / count
    first = jnp.where(gx == 0, 1.0, 0.0)
    final = jnp.where(gx == 3, 1.0, 0.0)
    on_diagonal = row == column
    load_diag.wait()
    load_sigma.wait()
    load_rates.wait()
    rate = BROADENING + (first * rates[0] + final * rates[1])
    own[0] = jnp.where(on_diagonal, energy, 0.0) - diag[0, 0] - sigma[0, 0, 0]
    own[1] = jnp.where(on_diagonal, rate, 0.0) - diag[1, 0] - sigma[1, 0, 0]
    work[...] = own[...]
    load_coupling.wait()
    pl.semaphore_wait(barrier, waits)
    send_piece.start()
    send_near.start()

    @pl.when(even)
    def _():
        store(step_in, adjoint((coupling[0, 0], coupling[1, 0])))
        store(step_out, (coupling[0, 0], coupling[1, 0]))

    def level(number, carry):
        def share_coupling():
            @pl.when(number == 0)
            def _():
                send_piece.wait_recv()
                for step in range(1, SHARE):
                    hand_on(step, place).start()

        invert(work, share_coupling)

        @pl.when(number == 0)
        def _():
            for step in range(1, SHARE):
                hand_on(step, lax.rem(place + SHARE - step, SHARE)).wait_recv()

            @pl.when(odd)
            def _():
                store(step_in, pair_of(link))
                store(step_out, adjoint(pair_of(link)))

            send_near.wait_send()
            g = pair_of(work)
            store(own, g)
            through = multiply(pair_of(step_in), g)
            store(reached, through)
            part = multiply(through, pair_of(step_out))
            send_near.wait_recv()
            pivot = subtract(pair_of(near), part)
            store(work, pivot)

            @pl.when(outer)
            def _():
                store(sent, pivot)
                send_mid.start()
                store(mid, pivot)

            @pl.when(gx == 0)
            def _():
                store(bridge, pair_of(link))

            @pl.when(gx == 1)
            def _():
                store(bridge, (coupling[0, 0], coupling[1, 0]))

            @pl.when(left)
            def _():
                store(bridge_h, adjoint(pair_of(bridge)))

            @pl.when(inner)
            def _():
                store(step_out, multiply(g, pair_of(step_out)))

        @pl.when(number == 1)
        def _():
            @pl.when(inner)
            def _():
                change = multiply(multiply(pair_of(step_out), pair_of(work)), pair_of(reached))
                store(work, addition(pair_of(own), change))

            @pl.when(outer)
            def _():
                send_mid.wait_send()

            @pl.when(left)
            def _():
                store(sent, multiply(pair_of(bridge_h), multiply(pair_of(work), pair_of(bridge))))

            @pl.when(right)
            def _():
                store(sent, pair_of(work))

            send_across.start()

            @pl.when(outer)
            def _():
                store(step_out, multiply(pair_of(own), pair_of(step_out)))

            @pl.when(inner)
            def _():
                send_mid.wait_recv()

            send_across.wait_recv()

        @pl.when((number == 1) & left)
        def _():
            reach = multiply(multiply(pair_of(bridge), pair_of(far)), pair_of(bridge_h))
            store(work, subtract(pair_of(mid), reach))

        @pl.when((number == 1) & right)
        def _():
            store(work, subtract(pair_of(mid), pair_of(far)))

        return carry

    lax.fori_loop(0, 3, level, 0)

    @pl.when(outer)
    def _():
        change = multiply(multiply(pair_of(step_out), pair_of(work)), pair_of(reached))
        store(last, addition(pair_of(own), change))

    @pl.when(inner)
    def _():
        store(last, pair_of(work))

    @pl.when(ea < count - 1)
    def _():
        send_up.start()

    @pl.when(ea > 0)
    def _():
        send_down.start()

    @pl.when(ea == 0)
    def _():
        before[...] = jnp.zeros_like(before)

    @pl.when(ea == count - 1)
    def _():
        after[...] = jnp.zeros_like(after)

    send_piece.wait_send()
    for step in range(1, SHARE):
        hand_on(step, place).wait_send()
    send_across.wait_send()
    load_form.wait()

    @pl.when(ea > 0)
    def _():
        send_up.wait_recv()

    @pl.when(ea < count - 1)
    def _():
        send_down.wait_recv()

    for c in range(2):
        out_ref[c, 0, 0] = form[...] * (before[c] + after[c])

    @pl.when(ea < count - 1)
    def _():
        send_up.wait_send()

    @pl.when(ea > 0)
    def _():
        send_down.wait_send()


def per_device(ham_diag, ham_coupling, sigma_prev, phonon_form, contact_rate):
    operands = (ham_diag, ham_coupling, sigma_prev, phonon_form, contact_rate)
    block = pltpu.VMEM((2, N, N), jnp.float32)
    return pl.pallas_call(
        kernel,
        out_shape=jax.ShapeDtypeStruct(sigma_prev.shape, jnp.float32),
        in_specs=[pl.BlockSpec(memory_space=pl.ANY)] * 5,
        out_specs=pl.BlockSpec(memory_space=pltpu.VMEM),
        scratch_shapes=[pltpu.VMEM(x.shape, jnp.float32) for x in operands]
        + [block] * 15
        + [pltpu.SemaphoreType.DMA((n,)) for n in (5, 6, 6, SHARE, SHARE)],
        compiler_params=pltpu.CompilerParams(
            collective_id=0, has_side_effects=True, vmem_limit_bytes=60 << 20
        ),
        name="born_update",
    )(*operands)


def solution(mesh):
    placed = (
        P(None, "gx", None, None),
        P(None, "gx", None, None),
        P(None, "gx", "ea", None, None),
        P(),
        P(None, "ea", None),
    )
    return jax.shard_map(
        per_device,
        mesh=mesh,
        in_specs=placed,
        out_specs=P(None, "gx", "ea", None, None),
        check_vma=False,
    )
```

```python
import jax
import jax.numpy as jnp
from jax import lax
from jax.experimental import pallas as pl
from jax.experimental.pallas import tpu as pltpu
from jax.sharding import PartitionSpec as P

BROADENING = 0.05
ENERGY_LOW = -2.0
ENERGY_SPAN = 4.0
N = 128
TILE = (8, 128)
SHARE = 8
ROWS = N // SHARE
MESH = pl.DeviceIdType.MESH


def spread(x):
    return jnp.broadcast_to(x, TILE)


def split3(x):
    high = x.astype(jnp.bfloat16)
    rest = x - high.astype(jnp.float32)
    middle = rest.astype(jnp.bfloat16)
    low = (rest - middle.astype(jnp.float32)).astype(jnp.bfloat16)
    return high, middle, low


def dot16(a, b):
    return jnp.dot(a, b, preferred_element_type=jnp.float32)


def product6(left, right):
    lh, lm, ll = left
    rh, rm, rl = right
    small = (dot16(lm, rm) + dot16(lh, rl)) + dot16(ll, rh)
    return dot16(lh, rh) + ((dot16(lh, rm) + dot16(lm, rh)) + small)


def multiply(left, right):
    x = jnp.concatenate(left, axis=1)
    top = jnp.concatenate(right, axis=1)
    bottom = jnp.concatenate([-right[1], right[0]], axis=1)
    y = product6(split3(x), split3(jnp.concatenate([top, bottom], axis=0)))
    return y[:, :N], y[:, N:]


def adjoint(pair):
    return pair[0].T, -pair[1].T


def addition(left, right):
    return left[0] + right[0], left[1] + right[1]


def subtract(left, right):
    return left[0] - right[0], left[1] - right[1]


def pair_of(ref):
    return ref[0], ref[1]


def store(ref, pair):
    ref[0] = pair[0]
    ref[1] = pair[1]


def pivot_rows(t, rows):
    sub = lax.broadcasted_iota(jnp.int32, TILE, 0)
    lane = lax.broadcasted_iota(jnp.int32, TILE, 1)
    o = 8 * t
    cols = [(spread(rows[0][:, o + m : o + m + 1]), spread(rows[1][:, o + m : o + m + 1])) for m in range(8)]
    inside = (lane >= o) & (lane < o + 8)
    x = (
        jnp.where(inside, jnp.where(lane - o == sub, 1.0, 0.0), rows[0]),
        jnp.where(inside, 0.0, rows[1]),
    )
    for k in range(8):
        at = sub == k
        mr, mi = cols[k]
        pr, pi = spread(mr[k : k + 1]), spread(mi[k : k + 1])
        recip = 1.0 / (pr * pr + pi * pi)
        mr, mi = jnp.where(at, -1.0, mr), jnp.where(at, 0.0, mi)
        ur, ui = mr * pr + mi * pi, mi * pr - mr * pi
        wr, wi = ur * recip, ui * recip

        def step(v, next_pivot):
            rr, ri = spread(v[0][k : k + 1]), spread(v[1][k : k + 1])
            vr, vi = jnp.where(at, 0.0, v[0]), jnp.where(at, 0.0, v[1])
            if next_pivot:
                return vr - (ur * rr - ui * ri) * recip, vi - (ur * ri + ui * rr) * recip
            return vr - (wr * rr - wi * ri), vi - (wr * ri + wi * rr)

        for m in range(k + 1, 8):
            cols[m] = step(cols[m], m == k + 1)
        x = step(x, False)
    return x


def factors(rows, t):
    o = 8 * t
    return [(spread(rows[0][:, o + k : o + k + 1]), spread(rows[1][:, o + k : o + k + 1])) for k in range(8)]


def combine(columns, x):
    real, imag = [], []
    for k, (cr, ci) in enumerate(columns):
        rr, ri = spread(x[0][k : k + 1]), spread(x[1][k : k + 1])
        real.append(cr * rr - ci * ri)
        imag.append(cr * ri + ci * rr)
    while len(real) > 1:
        real = [a + b for a, b in zip(real[::2], real[1::2])]
        imag = [a + b for a, b in zip(imag[::2], imag[1::2])]
    return real[0], imag[0]


def cleared(rows, first, width):
    lane = lax.broadcasted_iota(jnp.int32, TILE, 1)
    inside = (lane >= first) & (lane < first + width)
    return jnp.where(inside, 0.0, rows[0]), jnp.where(inside, 0.0, rows[1])


def invert(ref, between=None):
    groups = N // 8
    a = [(ref[0, 8 * g : 8 * g + 8, :], ref[1, 8 * g : 8 * g + 8, :]) for g in range(groups)]
    for s in range(groups // 2):
        if between and s == 6:
            between()
        g0, g1 = 2 * s, 2 * s + 1
        ahead = [] if s == groups // 2 - 1 else [g1 + 1, g1 + 2]
        old = list(a)
        x0 = pivot_rows(g0, a[g0])
        x1 = pivot_rows(g1, subtract(cleared(a[g1], 8 * g0, 8), combine(factors(a[g1], g0), x0)))
        x0 = subtract(cleared(x0, 8 * g1, 8), combine(factors(x0, g1), x1))
        for h in ahead:
            part = subtract(cleared(old[h], 16 * s, 16), combine(factors(old[h], g1), x1))
            a[h] = subtract(part, combine(factors(old[h], g0), x0))
        a[g0], a[g1] = x0, x1
        done = [g0, g1] + ahead
        real = jnp.concatenate([x0[0], x1[0]], axis=0)
        imag = jnp.concatenate([x0[1], x1[1]], axis=0)
        top = split3(jnp.concatenate([real, imag], axis=1))
        bottom = split3(jnp.concatenate([-imag, real], axis=1))

        def placed(x):
            above = [jnp.zeros((16 * s, 2 * N), jnp.bfloat16)] if s else []
            below = [jnp.zeros((N - 16 * s - 16, 2 * N), jnp.bfloat16)] if ahead else []
            return above + [x] + below

        right = [jnp.concatenate(placed(u) + placed(v), axis=0) for u, v in zip(top, bottom)]
        left = jnp.concatenate(
            [jnp.concatenate([v[0] for v in old], axis=0), jnp.concatenate([v[1] for v in old], axis=0)], axis=1
        )
        change = product6(split3(left), right)
        for g in range(groups):
            if g not in done:
                rows = slice(8 * g, 8 * g + 8)
                a[g] = subtract(cleared(old[g], 16 * s, 16), (change[rows, :N], change[rows, N:]))
    for g in range(groups):
        ref[0, 8 * g : 8 * g + 8, :] = a[g][0]
        ref[1, 8 * g : 8 * g + 8, :] = a[g][1]


def kernel(
    diag_hbm, coupling_hbm, sigma_hbm, rate_hbm, out_ref,
    diag, coupling, sigma, rates,
    own, held, work, near, link, mid, bridge, bridge_h, step_in, step_out, onward, reached, sent, far, last, before, after,
    load_sem, send_sem, recv_sem, pass_sem, piece_sem,
):
    gx = lax.axis_index("gx")
    ea = lax.axis_index("ea")
    count = lax.axis_size("ea")
    left = gx < 2
    right = jnp.logical_not(left)
    outer = (gx == 0) | (gx == 3)
    inner = jnp.logical_not(outer)
    even = lax.rem(gx, 2) == 0
    odd = jnp.logical_not(even)
    partner = gx + 1 - 2 * lax.rem(gx, 2)
    across = 3 - gx
    place = lax.rem(ea, SHARE)
    base = ea - place

    def load(at, src, dst):
        return pltpu.make_async_copy(src, dst, load_sem.at[at])

    load_diag = load(0, diag_hbm, diag)
    load_sigma = load(1, sigma_hbm, sigma)
    load_rates = load(2, rate_hbm, rates)
    load_coupling = load(3, coupling_hbm, coupling)
    for one_load in (load_diag, load_sigma, load_rates, load_coupling):
        one_load.start()

    def copy(src, dst, at, to_gx, to_ea):
        return pltpu.make_async_remote_copy(
            src_ref=src,
            dst_ref=dst,
            send_sem=send_sem.at[at],
            recv_sem=recv_sem.at[at],
            device_id=(to_gx, to_ea),
            device_id_type=MESH,
        )

    def piece(ref, index):
        return ref.at[:, pl.ds(pl.multiple_of(index * ROWS, ROWS), ROWS), :]

    send_near = copy(own, near, 0, partner, ea)
    send_piece = copy(piece(coupling.at[:, 0], place), piece(link, place), 1, partner, ea)
    send_across = copy(sent, far, 2, across, ea)
    send_up = copy(last, before, 3, gx, lax.rem(ea + 1, count))
    send_down = copy(last, after, 4, gx, lax.rem(ea + count - 1, count))

    def hand_on(step, owner):
        return pltpu.make_async_remote_copy(
            src_ref=piece(link, owner),
            dst_ref=piece(link, owner),
            send_sem=pass_sem.at[step],
            recv_sem=piece_sem.at[step],
            device_id=(gx, base + lax.rem(place + step, SHARE)),
            device_id_type=MESH,
        )

    barrier = pltpu.get_barrier_semaphore()

    def greet(to_gx, to_ea):
        pl.semaphore_signal(barrier, inc=1, device_id=(to_gx, to_ea), device_id_type=MESH)

    greet(partner, ea)
    greet(across, ea)
    for step in range(1, SHARE):
        greet(gx, base + lax.rem(place + step, SHARE))

    @pl.when(ea > 0)
    def _():
        greet(gx, ea - 1)

    @pl.when(ea < count - 1)
    def _():
        greet(gx, ea + 1)

    waits = 1 + SHARE + jnp.where(ea > 0, 1, 0) + jnp.where(ea < count - 1, 1, 0)

    row = lax.broadcasted_iota(jnp.int32, (N, N), 0)
    column = lax.broadcasted_iota(jnp.int32, (N, N), 1)
    energy = ENERGY_LOW + ENERGY_SPAN * (ea.astype(jnp.float32) + 0.5) / count
    first = jnp.where(gx == 0, 1.0, 0.0)
    final = jnp.where(gx == 3, 1.0, 0.0)
    on_diagonal = row == column
    load_diag.wait()
    load_sigma.wait()
    load_rates.wait()
    rate = BROADENING + (first * rates[0] + final * rates[1])
    own[0] = jnp.where(on_diagonal, energy, 0.0) - diag[0, 0] - sigma[0, 0, 0]
    own[1] = jnp.where(on_diagonal, rate, 0.0) - diag[1, 0] - sigma[1, 0, 0]
    work[...] = own[...]
    load_coupling.wait()
    pl.semaphore_wait(barrier, waits)
    send_piece.start()
    send_near.start()

    @pl.when(even)
    def _():
        store(step_in, adjoint((coupling[0, 0], coupling[1, 0])))
        store(step_out, (coupling[0, 0], coupling[1, 0]))

    def share_coupling():
        send_piece.wait_recv()
        for step in range(1, SHARE):
            hand_on(step, place).start()

    invert(work, share_coupling)

    for step in range(1, SHARE):
        hand_on(step, lax.rem(place + SHARE - step, SHARE)).wait_recv()

    @pl.when(odd)
    def _():
        store(step_in, pair_of(link))
        store(step_out, adjoint(pair_of(link)))

    @pl.when(gx == 0)
    def _():
        store(bridge, pair_of(link))

    @pl.when(gx == 1)
    def _():
        store(bridge, (coupling[0, 0], coupling[1, 0]))

    @pl.when(left)
    def _():
        store(bridge_h, adjoint(pair_of(bridge)))

    g = pair_of(work)
    through = multiply(pair_of(step_in), g)
    store(reached, through)
    part = multiply(through, pair_of(step_out))
    send_near.wait_recv()
    pivot = subtract(pair_of(near), part)
    store(held, g)
    store(work, pivot)

    @pl.when(outer)
    def _():
        store(mid, pivot)

    @pl.when(inner)
    def _():
        store(onward, multiply(pair_of(held), pair_of(step_out)))

    def level(number, carry):
        @pl.when(inner | (number != 2))
        def _():
            invert(work)

        @pl.when(number == 1)
        def _():
            @pl.when(inner)
            def _():
                change = multiply(multiply(pair_of(onward), pair_of(work)), pair_of(reached))
                store(work, addition(pair_of(held), change))

            @pl.when(left)
            def _():
                store(sent, multiply(pair_of(bridge_h), multiply(pair_of(work), pair_of(bridge))))

            @pl.when(right)
            def _():
                store(sent, pair_of(work))

            send_across.start()

            @pl.when(outer)
            def _():
                store(onward, multiply(pair_of(held), pair_of(step_out)))

            @pl.when(inner)
            def _():
                store(work, pair_of(near))

        @pl.when(inner & (number == 2))
        def _():
            part = multiply(multiply(pair_of(step_out), pair_of(work)), pair_of(step_in))
            store(mid, subtract(pair_of(own), part))

        @pl.when(number == 2)
        def _():
            send_across.wait_recv()

        @pl.when((number == 2) & left)
        def _():
            reach = multiply(multiply(pair_of(bridge), pair_of(far)), pair_of(bridge_h))
            store(work, subtract(pair_of(mid), reach))

        @pl.when((number == 2) & right)
        def _():
            store(work, subtract(pair_of(mid), pair_of(far)))

        return carry

    lax.fori_loop(1, 4, level, 0)

    @pl.when(outer)
    def _():
        change = multiply(multiply(pair_of(onward), pair_of(work)), pair_of(reached))
        store(last, addition(pair_of(held), change))

    @pl.when(inner)
    def _():
        store(last, pair_of(work))

    @pl.when(ea < count - 1)
    def _():
        send_up.start()

    @pl.when(ea > 0)
    def _():
        send_down.start()

    @pl.when(ea == 0)
    def _():
        before[...] = jnp.zeros_like(before)

    @pl.when(ea == count - 1)
    def _():
        after[...] = jnp.zeros_like(after)

    send_near.wait_send()
    send_piece.wait_send()
    for step in range(1, SHARE):
        hand_on(step, place).wait_send()
    send_across.wait_send()

    @pl.when(ea > 0)
    def _():
        send_up.wait_recv()

    @pl.when(ea < count - 1)
    def _():
        send_down.wait_recv()

    for c in range(2):
        out_ref[c, 0, 0] = before[c] + after[c]

    @pl.when(ea < count - 1)
    def _():
        send_up.wait_send()

    @pl.when(ea > 0)
    def _():
        send_down.wait_send()


def per_device(ham_diag, ham_coupling, sigma_prev, phonon_form, contact_rate):
    operands = (ham_diag, ham_coupling, sigma_prev, contact_rate)
    block = pltpu.VMEM((2, N, N), jnp.float32)
    total = pl.pallas_call(
        kernel,
        out_shape=jax.ShapeDtypeStruct(sigma_prev.shape, jnp.float32),
        in_specs=[pl.BlockSpec(memory_space=pl.ANY)] * 4,
        out_specs=pl.BlockSpec(memory_space=pltpu.VMEM),
        scratch_shapes=[pltpu.VMEM(x.shape, jnp.float32) for x in operands]
        + [block] * 17
        + [pltpu.SemaphoreType.DMA((n,)) for n in (4, 5, 5, SHARE, SHARE)],
        compiler_params=pltpu.CompilerParams(
            collective_id=0, has_side_effects=True, vmem_limit_bytes=(53 << 20) + (800 << 10)
        ),
        name="born_update",
    )(*operands)
    return phonon_form * total


def solution(mesh):
    placed = (
        P(None, "gx", None, None),
        P(None, "gx", None, None),
        P(None, "gx", "ea", None, None),
        P(),
        P(None, "ea", None),
    )
    return jax.shard_map(
        per_device,
        mesh=mesh,
        in_specs=placed,
        out_specs=P(None, "gx", "ea", None, None),
        check_vma=False,
    )
```

```python
import jax
import jax.numpy as jnp
from jax import lax
from jax.experimental import pallas as pl
from jax.experimental.pallas import tpu as pltpu
from jax.sharding import PartitionSpec as P

BROADENING = 0.05
ENERGY_LOW = -2.0
ENERGY_SPAN = 4.0
N = 128
TILE = (8, 128)
SHARE = 2
ROWS = N // SHARE
MESH = pl.DeviceIdType.MESH


def spread(x):
    return jnp.broadcast_to(x, TILE)


def split3(x):
    high = x.astype(jnp.bfloat16)
    rest = x - high.astype(jnp.float32)
    middle = rest.astype(jnp.bfloat16)
    low = (rest - middle.astype(jnp.float32)).astype(jnp.bfloat16)
    return high, middle, low


def dot16(a, b):
    return jnp.dot(a, b, preferred_element_type=jnp.float32)


def product6(left, right):
    lh, lm, ll = left
    rh, rm, rl = right
    small = (dot16(lm, rm) + dot16(lh, rl)) + dot16(ll, rh)
    return dot16(lh, rh) + ((dot16(lh, rm) + dot16(lm, rh)) + small)


def multiply(left, right):
    x = jnp.concatenate(left, axis=1)
    top = jnp.concatenate(right, axis=1)
    bottom = jnp.concatenate([-right[1], right[0]], axis=1)
    y = product6(split3(x), split3(jnp.concatenate([top, bottom], axis=0)))
    return y[:, :N], y[:, N:]


def adjoint(pair):
    return pair[0].T, -pair[1].T


def addition(left, right):
    return left[0] + right[0], left[1] + right[1]


def subtract(left, right):
    return left[0] - right[0], left[1] - right[1]


def pair_of(ref):
    return ref[0], ref[1]


def store(ref, pair):
    ref[0] = pair[0]
    ref[1] = pair[1]


def pivot_rows(t, rows):
    sub = lax.broadcasted_iota(jnp.int32, TILE, 0)
    lane = lax.broadcasted_iota(jnp.int32, TILE, 1)
    o = 8 * t
    cols = [(spread(rows[0][:, o + m : o + m + 1]), spread(rows[1][:, o + m : o + m + 1])) for m in range(8)]
    inside = (lane >= o) & (lane < o + 8)
    x = (
        jnp.where(inside, jnp.where(lane - o == sub, 1.0, 0.0), rows[0]),
        jnp.where(inside, 0.0, rows[1]),
    )
    for k in range(8):
        at = sub == k
        mr, mi = cols[k]
        pr, pi = spread(mr[k : k + 1]), spread(mi[k : k + 1])
        recip = 1.0 / (pr * pr + pi * pi)
        mr, mi = jnp.where(at, -1.0, mr), jnp.where(at, 0.0, mi)
        ur, ui = mr * pr + mi * pi, mi * pr - mr * pi
        wr, wi = ur * recip, ui * recip

        def step(v, next_pivot):
            rr, ri = spread(v[0][k : k + 1]), spread(v[1][k : k + 1])
            vr, vi = jnp.where(at, 0.0, v[0]), jnp.where(at, 0.0, v[1])
            if next_pivot:
                return vr - (ur * rr - ui * ri) * recip, vi - (ur * ri + ui * rr) * recip
            return vr - (wr * rr - wi * ri), vi - (wr * ri + wi * rr)

        for m in range(k + 1, 8):
            cols[m] = step(cols[m], m == k + 1)
        x = step(x, False)
    return x


def factors(rows, t):
    o = 8 * t
    return [(spread(rows[0][:, o + k : o + k + 1]), spread(rows[1][:, o + k : o + k + 1])) for k in range(8)]


def combine(columns, x):
    real, imag = [], []
    for k, (cr, ci) in enumerate(columns):
        rr, ri = spread(x[0][k : k + 1]), spread(x[1][k : k + 1])
        real.append(cr * rr - ci * ri)
        imag.append(cr * ri + ci * rr)
    while len(real) > 1:
        real = [a + b for a, b in zip(real[::2], real[1::2])]
        imag = [a + b for a, b in zip(imag[::2], imag[1::2])]
    return real[0], imag[0]


def cleared(rows, first, width):
    lane = lax.broadcasted_iota(jnp.int32, TILE, 1)
    inside = (lane >= first) & (lane < first + width)
    return jnp.where(inside, 0.0, rows[0]), jnp.where(inside, 0.0, rows[1])


def invert(ref):
    groups = N // 8
    a = [(ref[0, 8 * g : 8 * g + 8, :], ref[1, 8 * g : 8 * g + 8, :]) for g in range(groups)]
    for s in range(groups // 2):
        g0, g1 = 2 * s, 2 * s + 1
        ahead = [] if s == groups // 2 - 1 else [g1 + 1, g1 + 2]
        old = list(a)
        x0 = pivot_rows(g0, a[g0])
        x1 = pivot_rows(g1, subtract(cleared(a[g1], 8 * g0, 8), combine(factors(a[g1], g0), x0)))
        x0 = subtract(cleared(x0, 8 * g1, 8), combine(factors(x0, g1), x1))
        for h in ahead:
            part = subtract(cleared(old[h], 16 * s, 16), combine(factors(old[h], g1), x1))
            a[h] = subtract(part, combine(factors(old[h], g0), x0))
        a[g0], a[g1] = x0, x1
        done = [g0, g1] + ahead
        real = jnp.concatenate([x0[0], x1[0]], axis=0)
        imag = jnp.concatenate([x0[1], x1[1]], axis=0)
        top = split3(jnp.concatenate([real, imag], axis=1))
        bottom = split3(jnp.concatenate([-imag, real], axis=1))

        def placed(x):
            above = [jnp.zeros((16 * s, 2 * N), jnp.bfloat16)] if s else []
            below = [jnp.zeros((N - 16 * s - 16, 2 * N), jnp.bfloat16)] if ahead else []
            return above + [x] + below

        right = [jnp.concatenate(placed(u) + placed(v), axis=0) for u, v in zip(top, bottom)]
        left = jnp.concatenate(
            [jnp.concatenate([v[0] for v in old], axis=0), jnp.concatenate([v[1] for v in old], axis=0)], axis=1
        )
        change = product6(split3(left), right)
        for g in range(groups):
            if g not in done:
                rows = slice(8 * g, 8 * g + 8)
                a[g] = subtract(cleared(old[g], 16 * s, 16), (change[rows, :N], change[rows, N:]))
    for g in range(groups):
        ref[0, 8 * g : 8 * g + 8, :] = a[g][0]
        ref[1, 8 * g : 8 * g + 8, :] = a[g][1]


def kernel(
    diag_hbm, coupling_hbm, sigma_hbm, rate_hbm, out_ref,
    diag, coupling, sigma, rates,
    own, held, work, near, link, mid, bridge, bridge_h, step_in, step_out, onward, reached, sent, far, last, before, after,
    load_sem, send_sem, recv_sem, pass_sem, piece_sem,
):
    gx = lax.axis_index("gx")
    ea = lax.axis_index("ea")
    count = lax.axis_size("ea")
    left = gx < 2
    right = jnp.logical_not(left)
    outer = (gx == 0) | (gx == 3)
    inner = jnp.logical_not(outer)
    even = lax.rem(gx, 2) == 0
    odd = jnp.logical_not(even)
    partner = gx + 1 - 2 * lax.rem(gx, 2)
    across = 3 - gx
    place = lax.rem(ea, SHARE)
    base = ea - place

    def load(at, src, dst):
        return pltpu.make_async_copy(src, dst, load_sem.at[at])

    load_diag = load(0, diag_hbm, diag)
    load_sigma = load(1, sigma_hbm, sigma)
    load_rates = load(2, rate_hbm, rates)
    load_coupling = load(3, coupling_hbm, coupling)
    for one_load in (load_diag, load_sigma, load_rates, load_coupling):
        one_load.start()

    def copy(src, dst, at, to_gx, to_ea):
        return pltpu.make_async_remote_copy(
            src_ref=src,
            dst_ref=dst,
            send_sem=send_sem.at[at],
            recv_sem=recv_sem.at[at],
            device_id=(to_gx, to_ea),
            device_id_type=MESH,
        )

    def piece(ref, index):
        return ref.at[:, pl.ds(pl.multiple_of(index * ROWS, ROWS), ROWS), :]

    send_near = copy(own, near, 0, partner, ea)
    send_piece = copy(piece(coupling.at[:, 0], place), piece(link, place), 1, partner, ea)
    send_across = copy(sent, far, 2, across, ea)
    send_up = copy(last, before, 3, gx, lax.rem(ea + 1, count))
    send_down = copy(last, after, 4, gx, lax.rem(ea + count - 1, count))

    def hand_on(step, owner):
        return pltpu.make_async_remote_copy(
            src_ref=piece(link, owner),
            dst_ref=piece(link, owner),
            send_sem=pass_sem.at[step],
            recv_sem=piece_sem.at[step],
            device_id=(gx, base + lax.rem(place + step, SHARE)),
            device_id_type=MESH,
        )

    barrier = pltpu.get_barrier_semaphore()

    def greet(to_gx, to_ea):
        pl.semaphore_signal(barrier, inc=1, device_id=(to_gx, to_ea), device_id_type=MESH)

    greet(partner, ea)
    greet(across, ea)
    for step in range(1, SHARE):
        greet(gx, base + lax.rem(place + step, SHARE))

    @pl.when(ea > 0)
    def _():
        greet(gx, ea - 1)

    @pl.when(ea < count - 1)
    def _():
        greet(gx, ea + 1)

    waits = 1 + SHARE + jnp.where(ea > 0, 1, 0) + jnp.where(ea < count - 1, 1, 0)

    row = lax.broadcasted_iota(jnp.int32, (N, N), 0)
    column = lax.broadcasted_iota(jnp.int32, (N, N), 1)
    energy = ENERGY_LOW + ENERGY_SPAN * (ea.astype(jnp.float32) + 0.5) / count
    first = jnp.where(gx == 0, 1.0, 0.0)
    final = jnp.where(gx == 3, 1.0, 0.0)
    on_diagonal = row == column
    load_diag.wait()
    load_sigma.wait()
    load_rates.wait()
    rate = BROADENING + (first * rates[0] + final * rates[1])
    own[0] = jnp.where(on_diagonal, energy, 0.0) - diag[0, 0] - sigma[0, 0, 0]
    own[1] = jnp.where(on_diagonal, rate, 0.0) - diag[1, 0] - sigma[1, 0, 0]
    work[...] = own[...]
    load_coupling.wait()
    pl.semaphore_wait(barrier, waits)
    send_piece.start()
    send_near.start()

    @pl.when(even)
    def _():
        store(step_in, adjoint((coupling[0, 0], coupling[1, 0])))
        store(step_out, (coupling[0, 0], coupling[1, 0]))

    invert(work)
    send_piece.wait_recv()
    for step in range(1, SHARE):
        hand_on(step, place).start()

    for step in range(1, SHARE):
        hand_on(step, lax.rem(place + SHARE - step, SHARE)).wait_recv()

    @pl.when(odd)
    def _():
        store(step_in, pair_of(link))
        store(step_out, adjoint(pair_of(link)))

    @pl.when(gx == 0)
    def _():
        store(bridge, pair_of(link))

    @pl.when(gx == 1)
    def _():
        store(bridge, (coupling[0, 0], coupling[1, 0]))

    @pl.when(left)
    def _():
        store(bridge_h, adjoint(pair_of(bridge)))

    g = pair_of(work)
    through = multiply(pair_of(step_in), g)
    store(reached, through)
    part = multiply(through, pair_of(step_out))
    send_near.wait_recv()
    pivot = subtract(pair_of(near), part)
    store(held, g)
    store(work, pivot)

    @pl.when(outer)
    def _():
        store(mid, pivot)

    @pl.when(inner)
    def _():
        store(onward, multiply(pair_of(held), pair_of(step_out)))

    def level(number, carry):
        @pl.when(inner | (number != 2))
        def _():
            invert(work)

        @pl.when(number == 1)
        def _():
            @pl.when(inner)
            def _():
                change = multiply(multiply(pair_of(onward), pair_of(work)), pair_of(reached))
                store(work, addition(pair_of(held), change))

            @pl.when(left)
            def _():
                store(sent, multiply(pair_of(bridge_h), multiply(pair_of(work), pair_of(bridge))))

            @pl.when(right)
            def _():
                store(sent, pair_of(work))

            send_across.start()

            @pl.when(outer)
            def _():
                store(onward, multiply(pair_of(held), pair_of(step_out)))

            @pl.when(inner)
            def _():
                store(work, pair_of(near))

        @pl.when(inner & (number == 2))
        def _():
            part = multiply(multiply(pair_of(step_out), pair_of(work)), pair_of(step_in))
            store(mid, subtract(pair_of(own), part))

        @pl.when(number == 2)
        def _():
            send_across.wait_recv()

        @pl.when((number == 2) & left)
        def _():
            reach = multiply(multiply(pair_of(bridge), pair_of(far)), pair_of(bridge_h))
            store(work, subtract(pair_of(mid), reach))

        @pl.when((number == 2) & right)
        def _():
            store(work, subtract(pair_of(mid), pair_of(far)))

        return carry

    lax.fori_loop(1, 4, level, 0)

    @pl.when(outer)
    def _():
        change = multiply(multiply(pair_of(onward), pair_of(work)), pair_of(reached))
        store(last, addition(pair_of(held), change))

    @pl.when(inner)
    def _():
        store(last, pair_of(work))

    @pl.when(ea < count - 1)
    def _():
        send_up.start()

    @pl.when(ea > 0)
    def _():
        send_down.start()

    @pl.when(ea == 0)
    def _():
        before[...] = jnp.zeros_like(before)

    @pl.when(ea == count - 1)
    def _():
        after[...] = jnp.zeros_like(after)

    send_near.wait_send()
    send_piece.wait_send()
    for step in range(1, SHARE):
        hand_on(step, place).wait_send()
    send_across.wait_send()

    @pl.when(ea > 0)
    def _():
        send_up.wait_recv()

    @pl.when(ea < count - 1)
    def _():
        send_down.wait_recv()

    for c in range(2):
        out_ref[c, 0, 0] = before[c] + after[c]

    @pl.when(ea < count - 1)
    def _():
        send_up.wait_send()

    @pl.when(ea > 0)
    def _():
        send_down.wait_send()


def per_device(ham_diag, ham_coupling, sigma_prev, phonon_form, contact_rate):
    operands = (ham_diag, ham_coupling, sigma_prev, contact_rate)
    block = pltpu.VMEM((2, N, N), jnp.float32)
    total = pl.pallas_call(
        kernel,
        out_shape=jax.ShapeDtypeStruct(sigma_prev.shape, jnp.float32),
        in_specs=[pl.BlockSpec(memory_space=pl.ANY)] * 4,
        out_specs=pl.BlockSpec(memory_space=pltpu.VMEM),
        scratch_shapes=[pltpu.VMEM(x.shape, jnp.float32) for x in operands]
        + [block] * 17
        + [pltpu.SemaphoreType.DMA((n,)) for n in (4, 5, 5, SHARE, SHARE)],
        compiler_params=pltpu.CompilerParams(
            collective_id=0, has_side_effects=True, vmem_limit_bytes=(53 << 20) + (800 << 10)
        ),
        name="born_update",
    )(*operands)
    return phonon_form * total


def solution(mesh):
    placed = (
        P(None, "gx", None, None),
        P(None, "gx", None, None),
        P(None, "gx", "ea", None, None),
        P(),
        P(None, "ea", None),
    )
    return jax.shard_map(
        per_device,
        mesh=mesh,
        in_specs=placed,
        out_specs=P(None, "gx", "ea", None, None),
        check_vma=False,
    )
```
